32 devices in a mesh: group: 2 (over y), inline: 4 (over z), xline: 2 (over core), shot: 2 (over x).
Axes of the slice: x: 2, y: 2, z: 4, core: 2. Of those that a mesh axis runs over, the one named last changes fastest.
Arguments:
- vel2: float32 [64, 32, 128], P('inline', 'xline'), may hold values from 0.05 to 0.18
- adj_prev: float32 [4, 64, 32, 128], P(('group', 'shot'), 'inline', 'xline'), parts along dimension 0, may hold values from -6 to 6
- adj_now: float32 [4, 64, 32, 128], P(('group', 'shot'), 'inline', 'xline'), parts along dimension 0, may hold values from -6 to 6
- src_field: float32 [4, 8, 64, 32, 128], P(('group', 'shot'), None, 'inline', 'xline'), parts along dimension 0, may hold values from -6 to 6
- residual: float32 [4, 8, 1024], P(('group', 'shot')), parts along dimension 0, may hold values from -18 to 18
- rec_inline: int32 [4, 1024], P(('group', 'shot')), parts along dimension 0, may hold values from 0 to 63
- rec_xline: int32 [4, 1024], P(('group', 'shot')), parts along dimension 0, may hold values from 0 to 31
- src_inline: int32 [4], P(('group', 'shot')), parts along dimension 0, may hold values from 0 to 63
- src_xline: int32 [4], P(('group', 'shot')), parts along dimension 0, may hold values from 0 to 31
- lag_list: int32 [32], replicated, may hold values from -16 to 15, as said below
Outputs:
- dso_image: float32 [64, 64, 32, 128], P(('group', 'shot'), 'inline', 'xline'), parts along dimension 0
The draws below stay inside these ranges and needn't reach their ends.
There are 2 independent parts, one for each index of `group`. The reference program is written for one: setup_inputs(seed, part) draws one part's arguments, and reference() takes and returns one part's arrays. A program takes and returns all parts, laid end to end along the dimension named above; an argument that names none is the same for every part. Nothing has to cross between parts.
Inputs may be any that keep to these rules, and one draw needn't show every extreme that they name: lag_list holds each of the 32 offsets -16 .. 15 once, in an order drawn from the seed.
All inputs are finite; a program needn't handle non-finite values.
Results may differ from the reference program's by a relative error of at most 0.0003.
Values sent between devices are 32-bit elements; how exact they have to be, the bound alone decides.
A program may use at most 128 MiB of HBM per device.

```python
import math
import jax
import jax.numpy as jnp
from jax import lax

NZ = 128
NT = 8
NLAG = 32
NREC = 1024
SHOTS = 2
NI = 64
NX = 32


def draw_lag_list(key, part):
    key = jax.random.fold_in(key, 7)
    return (jax.random.permutation(key, NLAG) - NLAG // 2).astype(jnp.int32)


def plant(entries, own_key, smallest, largest):
    longest = entries.shape.index(max(entries.shape))
    spots = []
    for shift in (0, 1):
        where = [jax.random.randint(jax.random.fold_in(own_key, axis), (), 0, length) for axis, length in enumerate(entries.shape)]
        where[longest] = (where[longest] + shift) % entries.shape[longest]
        spots.append(tuple(where))
    return entries.at[spots[0]].set(smallest).at[spots[1]].set(largest)


def levels(key, shape, shards, smallest, high):
    factor_of, own = 1.0, jax.random.fold_in(key, 6)
    for axis_at, blocks in shards:
        steps = jnp.exp(jax.random.uniform(jax.random.fold_in(own, axis_at), (blocks,), jnp.float32, smallest / len(shards), high / len(shards)))
        factor_of = factor_of * jnp.repeat(steps, shape[axis_at] // blocks).reshape([-1 if axis == axis_at else 1 for axis in range(len(shape))])
    return factor_of


def gaussian(rng, shape, spread, most, pieces=(), held_as=jnp.bfloat16):
    drawn = jax.random.normal(rng, shape, jnp.float32) * spread
    if len(pieces) > 0:
        drawn = levels(rng, shape, pieces, -0.22, 0.18) * drawn
    return jnp.clip(drawn, min=-most, max=most).astype(held_as)


def setup_inputs(seed: int = 0, part: int = 0) -> dict:
    keys = jax.random.split(jax.random.key(seed), 11)
    own_keys = jax.random.split(jax.random.fold_in(keys[10], part), 11)
    return {
        "vel2": jnp.clip(jnp.exp(math.log(0.18) - 1.2809339 * jax.random.uniform(keys[0], (NI, NX, NZ), jnp.float32) ** levels(keys[0], (NI, NX, NZ), ((0, 4), (1, 2)), -0.2, 0.2)), 0.05, 0.18),
        "adj_prev": gaussian(own_keys[1], (SHOTS, NI, NX, NZ), 1.0, 6.0, ((0, 2), (1, 4), (2, 2)), jnp.float32),
        "adj_now": gaussian(own_keys[2], (SHOTS, NI, NX, NZ), 1.0, 6.0, ((0, 2), (1, 4), (2, 2)), jnp.float32),
        "src_field": gaussian(own_keys[3], (SHOTS, NT, NI, NX, NZ), 1.0, 6.0, ((0, 2), (2, 4), (3, 2)), jnp.float32),
        "residual": gaussian(own_keys[4], (SHOTS, NT, NREC), 3.0, 18.0, ((0, 2),), jnp.float32),
        "rec_inline": plant(jax.random.randint(own_keys[5], (SHOTS, NREC), 0, NI), jax.random.fold_in(own_keys[5], 1), 0, NI - 1).astype(jnp.int32),
        "rec_xline": plant(jax.random.randint(own_keys[6], (SHOTS, NREC), 0, NX), jax.random.fold_in(own_keys[6], 1), 0, NX - 1).astype(jnp.int32),
        "src_inline": jax.random.randint(own_keys[7], (SHOTS,), 0, NI).astype(jnp.int32),
        "src_xline": jax.random.randint(own_keys[8], (SHOTS,), 0, NX).astype(jnp.int32),
        "lag_list": draw_lag_list(jax.random.fold_in(keys[10], 71), part),
    }


stencil_weights = (-205.0 / 72.0, 8.0 / 5.0, -1.0 / 5.0, 8.0 / 315.0, -1.0 / 560.0)
mute_reach = 3
receiver_depth = 1


def stencil(padded):
    size_a, size_b, size_c = padded.shape
    centre = padded[4:size_a - 4, 4:size_b - 4, 4:size_c - 4]
    summed_up = 3.0 * stencil_weights[0] * centre
    for reach in range(1, 5):
        summed_up = summed_up + stencil_weights[reach] * (
            padded[4 + reach:size_a - 4 + reach, 4:size_b - 4, 4:size_c - 4]
            + padded[4 - reach:size_a - 4 - reach, 4:size_b - 4, 4:size_c - 4]
            + padded[4:size_a - 4, 4 + reach:size_b - 4 + reach, 4:size_c - 4]
            + padded[4:size_a - 4, 4 - reach:size_b - 4 - reach, 4:size_c - 4]
            + padded[4:size_a - 4, 4:size_b - 4, 4 + reach:size_c - 4 + reach]
            + padded[4:size_a - 4, 4:size_b - 4, 4 - reach:size_c - 4 - reach])
    return summed_up


def reference(vel2, adj_prev, adj_now, src_field, residual, rec_inline, rec_xline, src_inline, src_xline, lag_list):
    lag_reach = NLAG // 2
    row_cells = jnp.arange(NI, dtype=jnp.int32)[:, None]
    col_cells = jnp.arange(NX, dtype=jnp.int32)[None, :]
    depth_mask = (jnp.arange(NZ, dtype=jnp.int32) == receiver_depth).astype(jnp.float32)
    accumulated = jnp.zeros((NLAG, NI, NX, NZ), jnp.float32)
    for shot_k in range(SHOTS):
        inside = (jnp.abs(row_cells - src_inline[shot_k]) <= mute_reach) & (jnp.abs(col_cells - src_xline[shot_k]) <= mute_reach)
        mute_mask = 1.0 - inside.astype(jnp.float32)
        older = adj_prev[shot_k]
        current = adj_now[shot_k]
        for step in range(NT):
            surface = jnp.zeros((NI, NX), jnp.float32).at[rec_inline[shot_k], rec_xline[shot_k]].add(residual[shot_k, step])
            advanced = 2.0 * current - older + vel2 * (stencil(jnp.pad(current, 4)) + surface[:, :, None] * depth_mask)
            widened = jnp.pad(advanced, ((lag_reach, lag_reach), (0, 0), (0, 0)))
            source = src_field[shot_k, step] * mute_mask[:, :, None]

            def one_lag(offset):
                zero = jnp.zeros((), jnp.int32)
                return lax.dynamic_slice(widened, ((offset + lag_reach).astype(jnp.int32), zero, zero), (NI, NX, NZ))

            accumulated = accumulated + source[None] * jax.vmap(one_lag)(lag_list)
            older, current = current, advanced
    weights = jnp.abs(lag_list).astype(jnp.float32)
    return accumulated * weights[:, None, None, None]
```

```python
import functools

import jax
import jax.numpy as jnp
from jax import lax
from jax.experimental import pallas as pl
from jax.experimental.pallas import tpu as pltpu
from jax.sharding import PartitionSpec as P

NLAG = 32
REACH = NLAG // 2
SIDE = 8

stencil_weights = (-205.0 / 72.0, 8.0 / 5.0, -1.0 / 5.0, 8.0 / 315.0, -1.0 / 560.0)
mute_reach = 3
receiver_depth = 1
MESH = pl.DeviceIdType.MESH


def kernel(
    sizes,
    lags,
    src_at_inline,
    src_at_xline,
    vel2,
    adj_prev,
    adj_now,
    residual,
    rec_inline,
    rec_xline,
    src_field,
    out,
    *scratch,
):
    shots, n_inline, n_xline, rows, cols, depth, steps = sizes
    fields = [
        [scratch[s * (steps + 1) + t] for t in range(steps + 1)] for s in range(shots)
    ]
    (older0, src, surf, surf_send, surf_recv, load_sem, prev_send, prev_recv, now_send, now_recv,
     src_send, src_recv, z_send, z_recv, j_send, j_recv) = scratch[shots * (steps + 1):]
    me_shot = lax.axis_index("shot")
    me_in = lax.axis_index("inline")
    me_x = lax.axis_index("xline")
    has_low, has_high = me_in > 0, me_in < n_inline - 1
    has_left, has_right = me_x > 0, me_x < n_xline - 1
    tile_rows = pl.ds(REACH, rows)
    tile_cols = pl.ds(SIDE, cols)

    def partner(d):
        return {"shot": lax.rem(me_shot + d, shots)}

    barrier = pltpu.get_barrier_semaphore()

    def greet(where):
        pl.semaphore_signal(barrier, inc=1, device_id=where, device_id_type=MESH)

    @pl.when(has_low)
    def _():
        greet({"inline": me_in - 1})

    @pl.when(has_high)
    def _():
        greet({"inline": me_in + 1})

    @pl.when(has_left)
    def _():
        greet({"xline": me_x - 1})

    @pl.when(has_right)
    def _():
        greet({"xline": me_x + 1})

    for d in range(1, shots):
        greet(partner(d))

    load_src = pltpu.make_async_copy(src_field.at[0], src.at[0], load_sem)
    load_src.start()
    fields[0][0][tile_rows, tile_cols, :] = adj_now[0]
    older0[0] = adj_prev[0]

    near = 4

    def z_copy(s, t, which, here, there, count, step_to):
        ref = fields[s][t]
        return pltpu.make_async_remote_copy(
            src_ref=ref.at[pl.ds(here, count), tile_cols, :],
            dst_ref=ref.at[pl.ds(there, count), tile_cols, :],
            send_sem=z_send.at[s, t, which],
            recv_sem=z_recv.at[s, t, which],
            device_id={"inline": me_in + step_to},
            device_id_type=MESH,
        )

    def z_near(s, t):
        return [
            (has_low, has_high, z_copy(s, t, 0, REACH, REACH + rows, near, -1)),
            (has_high, has_low, z_copy(s, t, 1, REACH + rows - near, REACH - near, near, 1)),
        ]

    def z_far(s, t):
        return [
            (has_low, has_high,
             z_copy(s, t, 2, REACH + near, REACH + rows + near, rows - near, -1)),
            (has_high, has_low, z_copy(s, t, 3, REACH, REACH - rows, rows - near, 1)),
        ]

    def j_side(s, t):
        ref = fields[s][t]
        left = pltpu.make_async_remote_copy(
            src_ref=ref.at[tile_rows, pl.ds(SIDE, SIDE), :],
            dst_ref=ref.at[tile_rows, pl.ds(SIDE + cols, SIDE), :],
            send_sem=j_send.at[s, t, 0],
            recv_sem=j_recv.at[s, t, 0],
            device_id={"xline": me_x - 1},
            device_id_type=MESH,
        )
        right = pltpu.make_async_remote_copy(
            src_ref=ref.at[tile_rows, pl.ds(cols, SIDE), :],
            dst_ref=ref.at[tile_rows, pl.ds(0, SIDE), :],
            send_sem=j_send.at[s, t, 1],
            recv_sem=j_recv.at[s, t, 1],
            device_id={"xline": me_x + 1},
            device_id_type=MESH,
        )
        return [(has_left, has_right, left), (has_right, has_left, right)]

    started = []

    def start(copies):
        for sends, _, copy in copies:
            pl.when(sends)(copy.start)
        started.extend(copies)

    def await_recv(copies):
        for _, receives, copy in copies:
            pl.when(receives)(copy.wait_recv)

    pl.semaphore_wait(
        barrier,
        has_low.astype(jnp.int32) + has_high.astype(jnp.int32)
        + has_left.astype(jnp.int32) + has_right.astype(jnp.int32) + (shots - 1),
    )

    start(z_near(0, 0))
    start(j_side(0, 0))

    def to_shot(d, src_ref, dst_ref, send_sem, recv_sem):
        return pltpu.make_async_remote_copy(
            src_ref=src_ref, dst_ref=dst_ref, send_sem=send_sem, recv_sem=recv_sem,
            device_id=partner(d), device_id_type=MESH,
        )

    shot_copies = []

    def now_copy(d):
        return to_shot(
            d, fields[0][0].at[tile_rows, tile_cols, :],
            fields[shots - d][0].at[tile_rows, tile_cols, :],
            now_send.at[d], now_recv.at[shots - d])

    def prev_copy(d):
        return to_shot(d, older0.at[0], older0.at[shots - d], prev_send.at[d],
                       prev_recv.at[shots - d])

    def surf_copy(d):
        return to_shot(d, surf.at[0], surf.at[shots - d], surf_send.at[d],
                       surf_recv.at[shots - d])

    def src_copy(d, t):
        return to_shot(d, src.at[0, t], src.at[shots - d, t], src_send.at[d, t],
                       src_recv.at[shots - d, t])

    def start_shot(copy):
        copy.start()
        shot_copies.append(copy)

    for d in range(1, shots):
        start_shot(now_copy(d))
    for d in range(1, shots):
        start_shot(prev_copy(d))

    row_ids = me_in * rows + lax.broadcasted_iota(jnp.int32, (rows, 1), 0)
    col_ids = me_x * cols + lax.broadcasted_iota(jnp.int32, (cols, 1), 0)
    hit_rows = (rec_inline[...] == row_ids).astype(jnp.float32)
    hit_cols = (rec_xline[...] == col_ids).astype(jnp.float32)
    weighted = jnp.concatenate(
        [hit_rows * residual[0, t : t + 1, :] for t in range(steps)], axis=0
    )
    surf[0] = lax.dot_general(
        hit_cols, weighted, (((1,), (1,)), ((), ())),
        precision=lax.Precision.HIGHEST, preferred_element_type=jnp.float32,
    )
    for d in range(1, shots):
        start_shot(surf_copy(d))

    @pl.when(jnp.logical_not(has_low))
    def _():
        for s in range(shots):
            for t in range(steps + 1):
                fields[s][t][0:REACH, tile_cols, :] = jnp.zeros((REACH, cols, depth), jnp.float32)

    @pl.when(jnp.logical_not(has_high))
    def _():
        for s in range(shots):
            for t in range(steps + 1):
                fields[s][t][pl.ds(REACH + rows, REACH), tile_cols, :] = jnp.zeros(
                    (REACH, cols, depth), jnp.float32)

    @pl.when(jnp.logical_not(has_left))
    def _():
        for s in range(shots):
            for t in range(steps):
                fields[s][t][tile_rows, 0:SIDE, :] = jnp.zeros((rows, SIDE, depth), jnp.float32)

    @pl.when(jnp.logical_not(has_right))
    def _():
        for s in range(shots):
            for t in range(steps):
                fields[s][t][tile_rows, pl.ds(SIDE + cols, SIDE), :] = jnp.zeros(
                    (rows, SIDE, depth), jnp.float32)

    load_src.wait()
    at_inline, at_xline = src_at_inline[0], src_at_xline[0]
    cell_cols = me_x * cols + lax.broadcasted_iota(jnp.int32, (cols, depth), 0)
    col_inside = (jnp.abs(cell_cols - at_xline) <= mute_reach).astype(jnp.float32)
    for t in range(steps):
        def mute_row(i, carry):
            hit = (jnp.abs(me_in * rows + i - at_inline) <= mute_reach).astype(jnp.float32)
            src[0, t, i] = src[0, t, i] * (1.0 - hit * col_inside)
            return carry

        lax.fori_loop(0, rows, mute_row, 0)
        for d in range(1, shots):
            start_shot(src_copy(d, t))

    lanes = lax.broadcasted_iota(jnp.int32, (cols, depth), 1)

    def advance(s, t):
        now, new = fields[s][t], fields[s][t + 1]

        def one_row(i):
            at = REACH + i
            centre = now[at, tile_cols, :]
            total = 3.0 * stencil_weights[0] * centre
            for reach in range(1, 5):
                up = jnp.where(lanes >= reach, pltpu.roll(centre, reach, 1), 0.0)
                down = jnp.where(
                    lanes < depth - reach, pltpu.roll(centre, depth - reach, 1), 0.0)
                total = total + stencil_weights[reach] * (
                    (now[at + reach, tile_cols, :] + now[at - reach, tile_cols, :])
                    + (now[at, pl.ds(SIDE + reach, cols), :]
                       + now[at, pl.ds(SIDE - reach, cols), :])
                    + (up + down))
            shift = lax.rem(receiver_depth - (t * rows + i) + 2 * depth, depth)
            injected = jnp.where(
                lanes == receiver_depth, pltpu.roll(surf[s], shift, 1), 0.0)
            before = older0[s, i] if t == 0 else fields[s][t - 1][at, tile_cols, :]
            new[at, tile_cols, :] = 2.0 * centre - before + vel2[i] * (total + injected)

        def some_rows(b, carry):
            for i in range(4):
                one_row(b * 4 + i)
            return carry

        lax.fori_loop(0, rows // 4, some_rows, 0)

    own_count = NLAG // shots
    first_lag = me_shot * own_count

    def correlate(t):
        last = t == steps

        def one_row(i, carry):
            sources = [src[s, t - 1, i] for s in range(shots)]
            for k in range(own_count):
                lag = lags[first_lag + k]
                at = REACH + i + lag
                total = sources[0] * fields[0][t][at, tile_cols, :]
                for s in range(1, shots):
                    total = total + sources[s] * fields[s][t][at, tile_cols, :]
                if t > 1:
                    total = out[k, i] + total
                if last:
                    total = total * jnp.abs(lag).astype(jnp.float32)
                out[k, i] = total
            return carry

        lax.fori_loop(0, rows, one_row, 0)

    for t in range(steps):
        for s in range(shots):
            if t == 0 and s > 0:
                now_copy(shots - s).wait_recv()
                start(z_near(s, 0))
                start(j_side(s, 0))
        for s in range(shots):
            if t == 0 and s > 0:
                prev_copy(shots - s).wait_recv()
                surf_copy(shots - s).wait_recv()
            await_recv(j_side(s, t))
            await_recv(z_near(s, t))
            advance(s, t)
            start(z_near(s, t + 1))
            if t + 1 < steps:
                start(j_side(s, t + 1))
            start(z_far(s, t + 1))
        if t > 0:
            for s in range(shots):
                await_recv(z_far(s, t))
                if s > 0:
                    src_copy(shots - s, t - 1).wait_recv()
            correlate(t)
    for s in range(shots):
        await_recv(z_near(s, steps))
        await_recv(z_far(s, steps))
        if s > 0:
            src_copy(shots - s, steps - 1).wait_recv()
    correlate(steps)

    for sends, _, copy in started:
        pl.when(sends)(copy.wait_send)
    for copy in shot_copies:
        copy.wait_send()


def on_device(
    sizes,
    vel2,
    adj_prev,
    adj_now,
    src_field,
    residual,
    rec_inline,
    rec_xline,
    src_inline,
    src_xline,
    lag_list,
):
    shots, _, _, rows, cols, depth, steps = sizes
    vmem = pl.BlockSpec(memory_space=pltpu.VMEM)
    smem = pl.BlockSpec(memory_space=pltpu.SMEM)
    field = pltpu.VMEM((rows + 2 * REACH, cols + 2 * SIDE, depth), jnp.float32)
    dma = pltpu.SemaphoreType.DMA
    return pl.pallas_call(
        functools.partial(kernel, sizes),
        out_shape=jax.ShapeDtypeStruct((NLAG // shots, rows, cols, depth), jnp.float32),
        in_specs=[smem, smem, smem, vmem, vmem, vmem, vmem, vmem, vmem,
                  pl.BlockSpec(memory_space=pl.ANY)],
        out_specs=vmem,
        scratch_shapes=[field] * (shots * (steps + 1)) + [
            pltpu.VMEM((shots, rows, cols, depth), jnp.float32),
            pltpu.VMEM((shots, steps, rows, cols, depth), jnp.float32),
            pltpu.VMEM((shots, cols, depth), jnp.float32),
            dma((shots,)), dma((shots,)),
            dma,
            dma((shots,)), dma((shots,)),
            dma((shots,)), dma((shots,)),
            dma((shots, steps)), dma((shots, steps)),
            dma((shots, steps + 1, 4)), dma((shots, steps + 1, 4)),
            dma((shots, steps + 1, 2)), dma((shots, steps + 1, 2)),
        ],
        compiler_params=pltpu.CompilerParams(
            collective_id=0, has_side_effects=True, vmem_limit_bytes=52 * 2**20),
        name="adjoint_window",
    )(lag_list, src_inline, src_xline, vel2, adj_prev, adj_now, residual, rec_inline, rec_xline,
      src_field)


def solution(mesh):
    in_specs = (
        P("inline", "xline", None),
        P(("group", "shot"), "inline", "xline", None),
        P(("group", "shot"), "inline", "xline", None),
        P(("group", "shot"), None, "inline", "xline", None),
        P(("group", "shot"), None, None),
        P(("group", "shot"), None),
        P(("group", "shot"), None),
        P(("group", "shot")),
        P(("group", "shot")),
        P(),
    )
    out_specs = P(("group", "shot"), "inline", "xline", None)

    def whole(vel2, adj_prev, adj_now, src_field, *rest):
        n_inline, n_xline = mesh.shape["inline"], mesh.shape["xline"]
        sizes = (mesh.shape["shot"], n_inline, n_xline, vel2.shape[0] // n_inline,
                 vel2.shape[1] // n_xline, vel2.shape[2], src_field.shape[1])
        return jax.shard_map(
            functools.partial(on_device, sizes), mesh=mesh, in_specs=in_specs,
            out_specs=out_specs, check_vma=False,
        )(vel2, adj_prev, adj_now, src_field, *rest)

    return whole
```

```python
import functools

import jax
import jax.numpy as jnp
from jax import lax
from jax.experimental import pallas as pl
from jax.experimental.pallas import tpu as pltpu
from jax.sharding import PartitionSpec as P

NLAG = 32
REACH = NLAG // 2
NEAR = 4
EXTRA = REACH - NEAR
SIDE = 8

stencil_weights = (-205.0 / 72.0, 8.0 / 5.0, -1.0 / 5.0, 8.0 / 315.0, -1.0 / 560.0)
mute_reach = 3
receiver_depth = 1
MESH = pl.DeviceIdType.MESH


def kernel(
    sizes,
    lags_in,
    src_at_inline_in,
    src_at_xline_in,
    vel2_in,
    adj_prev_in,
    adj_now_in,
    residual_in,
    rec_inline_in,
    rec_xline_in,
    src_field,
    out,
    *scratch,
):
    shots, n_inline, n_xline, rows, cols, depth, steps = sizes
    fields = [
        [scratch[s * (steps + 1) + t] for t in range(steps + 1)] for s in range(shots)
    ]
    (lags, src_at_inline, src_at_xline, vel2, older0, residual, rec_inline, rec_xline,
     src, surf, load_sem, vel_send, vel_recv, surf_send, surf_recv, now_send, now_recv,
     src_send, src_recv, z_send, z_recv, j_send, j_recv) = scratch[shots * (steps + 1):]
    me_shot = lax.axis_index("shot")
    me_in = lax.axis_index("inline")
    me_x = lax.axis_index("xline")
    has_low, has_high = me_in > 0, me_in < n_inline - 1
    has_left, has_right = me_x > 0, me_x < n_xline - 1
    tile_rows = pl.ds(REACH, rows)
    tile_cols = pl.ds(SIDE, cols)

    loads = [
        pltpu.make_async_copy(src_ref, dst_ref, load_sem.at[n])
        for n, (src_ref, dst_ref) in enumerate([
            (adj_now_in.at[0], fields[0][0].at[tile_rows, tile_cols, :]),
            (adj_prev_in.at[0], older0),
            (vel2_in, vel2.at[tile_rows]),
            (residual_in.at[0], residual),
            (rec_inline_in, rec_inline),
            (rec_xline_in, rec_xline),
            (src_field.at[0], src.at[0]),
            (lags_in, lags),
            (src_at_inline_in, src_at_inline),
            (src_at_xline_in, src_at_xline),
        ])
    ]
    for load in loads:
        load.start()

    def partner(d):
        return {"shot": lax.rem(me_shot + d, shots)}

    barrier = pltpu.get_barrier_semaphore()

    def greet(where):
        pl.semaphore_signal(barrier, inc=1, device_id=where, device_id_type=MESH)

    @pl.when(has_low)
    def _():
        greet({"inline": me_in - 1})

    @pl.when(has_high)
    def _():
        greet({"inline": me_in + 1})

    @pl.when(has_left)
    def _():
        greet({"xline": me_x - 1})

    @pl.when(has_right)
    def _():
        greet({"xline": me_x + 1})

    for d in range(1, shots):
        greet(partner(d))

    def z_copy(s, t, which, here, there, count, step_to):
        ref = fields[s][t]
        return pltpu.make_async_remote_copy(
            src_ref=ref.at[pl.ds(here, count), tile_cols, :],
            dst_ref=ref.at[pl.ds(there, count), tile_cols, :],
            send_sem=z_send.at[s, t, which],
            recv_sem=z_recv.at[s, t, which],
            device_id={"inline": me_in + step_to},
            device_id_type=MESH,
        )

    def z_rows(s, t, which, begin, end):
        return [
            (has_low, has_high,
             z_copy(s, t, which, REACH + begin, REACH + rows + begin, end - begin, -1)),
            (has_high, has_low,
             z_copy(s, t, which + 1, REACH + rows - end, REACH - end, end - begin, 1)),
        ]

    def z_near(s, t):
        if t >= 3:
            return z_rows(s, t, 0, EXTRA, REACH)
        return z_rows(s, t, 0, 0, NEAR)

    def z_far(s, t):
        return z_rows(s, t, 2, NEAR, REACH)

    def z_vel():
        def one(which, here, there, step_to):
            return pltpu.make_async_remote_copy(
                src_ref=vel2.at[pl.ds(here, EXTRA)], dst_ref=vel2.at[pl.ds(there, EXTRA)],
                send_sem=vel_send.at[which], recv_sem=vel_recv.at[which],
                device_id={"inline": me_in + step_to}, device_id_type=MESH)

        return [(has_low, has_high, one(0, REACH, REACH + rows, -1)),
                (has_high, has_low, one(1, REACH + rows - EXTRA, REACH - EXTRA, 1))]

    def j_copy(s, t, which, begin, count):
        ref = fields[s][t]
        some_rows = pl.ds(begin, count)
        left = pltpu.make_async_remote_copy(
            src_ref=ref.at[some_rows, pl.ds(SIDE, SIDE), :],
            dst_ref=ref.at[some_rows, pl.ds(SIDE + cols, SIDE), :],
            send_sem=j_send.at[s, t, which],
            recv_sem=j_recv.at[s, t, which],
            device_id={"xline": me_x - 1},
            device_id_type=MESH,
        )
        right = pltpu.make_async_remote_copy(
            src_ref=ref.at[some_rows, pl.ds(cols, SIDE), :],
            dst_ref=ref.at[some_rows, pl.ds(0, SIDE), :],
            send_sem=j_send.at[s, t, which + 1],
            recv_sem=j_recv.at[s, t, which + 1],
            device_id={"xline": me_x + 1},
            device_id_type=MESH,
        )
        return [(has_left, has_right, left), (has_right, has_left, right)]

    def j_tile(s, t):
        return j_copy(s, t, 0, REACH, rows)

    def j_wide(s, t):
        return j_copy(s, t, 0, REACH - EXTRA, rows + 2 * EXTRA)

    started = []

    def start(copies):
        for sends, _, copy in copies:
            pl.when(sends)(copy.start)
        started.extend(copies)

    def await_recv(copies):
        for _, receives, copy in copies:
            pl.when(receives)(copy.wait_recv)

    shot_copies = []

    def to_shot(d, src_ref, dst_ref, send_sem, recv_sem):
        return pltpu.make_async_remote_copy(
            src_ref=src_ref, dst_ref=dst_ref, send_sem=send_sem, recv_sem=recv_sem,
            device_id=partner(d), device_id_type=MESH,
        )

    def field_copy(d, t):
        return to_shot(
            d, fields[0][t].at[tile_rows, tile_cols, :],
            fields[shots - d][t].at[tile_rows, tile_cols, :],
            now_send.at[d, t], now_recv.at[shots - d, t])

    def surf_copy(d):
        return to_shot(d, surf.at[0], surf.at[shots - d], surf_send.at[d],
                       surf_recv.at[shots - d])

    def src_copy(d, t):
        return to_shot(d, src.at[0, t], src.at[shots - d, t], src_send.at[d, t],
                       src_recv.at[shots - d, t])

    def to_shots(copy_of, *what):
        for d in range(1, shots):
            copy = copy_of(d, *what)
            copy.start()
            shot_copies.append(copy)

    @pl.when(jnp.logical_not(has_low))
    def _():
        zero = jnp.zeros((REACH, cols, depth), jnp.float32)
        vel2[0:REACH] = zero
        fields[0][0][0:REACH, tile_cols, :] = zero
        for s in range(shots):
            for t in range(1, steps + 1):
                upto = REACH if t < 3 else REACH - EXTRA
                fields[s][t][0:upto, tile_cols, :] = zero[:upto]

    @pl.when(jnp.logical_not(has_high))
    def _():
        zero = jnp.zeros((REACH, cols, depth), jnp.float32)
        vel2[pl.ds(REACH + rows, REACH)] = zero
        fields[0][0][pl.ds(REACH + rows, REACH), tile_cols, :] = zero
        for s in range(shots):
            for t in range(1, steps + 1):
                upto = REACH if t < 3 else REACH - EXTRA
                fields[s][t][pl.ds(2 * REACH + rows - upto, upto), tile_cols, :] = zero[:upto]

    def zero_side(begin):
        zero = jnp.zeros((rows + 2 * EXTRA, SIDE, depth), jnp.float32)
        for s in range(shots):
            for t in range(steps):
                fields[s][t][pl.ds(REACH - EXTRA, rows + 2 * EXTRA), pl.ds(begin, SIDE), :] = zero

    @pl.when(jnp.logical_not(has_left))
    def _():
        zero_side(0)

    @pl.when(jnp.logical_not(has_right))
    def _():
        zero_side(SIDE + cols)

    pl.semaphore_wait(
        barrier,
        has_low.astype(jnp.int32) + has_high.astype(jnp.int32)
        + has_left.astype(jnp.int32) + has_right.astype(jnp.int32) + (shots - 1),
    )
    loads[0].wait()
    start(z_near(0, 0))
    start(j_tile(0, 0))

    for load in loads[6:]:
        load.wait()
    at_inline, at_xline = src_at_inline[0], src_at_xline[0]
    cell_cols = me_x * cols + lax.broadcasted_iota(jnp.int32, (cols, depth), 0)
    col_inside = (jnp.abs(cell_cols - at_xline) <= mute_reach).astype(jnp.float32)

    def mute(t):
        def mute_row(i, carry):
            hit = (jnp.abs(me_in * rows + i - at_inline) <= mute_reach).astype(jnp.float32)
            src[0, t, i] = src[0, t, i] * (1.0 - hit * col_inside)
            return carry

        lax.fori_loop(0, rows, mute_row, 0)

    mute(0)
    to_shots(src_copy, 0)
    for load in loads[1:6]:
        load.wait()
    start(z_vel())

    col_ids = me_x * cols + lax.broadcasted_iota(jnp.int32, (cols, 1), 0)
    hit_cols = (rec_xline[...] == col_ids).astype(jnp.float32)

    def surface(tile):
        row_ids = (me_in + tile - 1) * rows + lax.broadcasted_iota(jnp.int32, (rows, 1), 0)
        hit_rows = (rec_inline[...] == row_ids).astype(jnp.float32)
        weighted = jnp.concatenate(
            [hit_rows * residual[t : t + 1, :] for t in range(steps)], axis=0
        )
        surf[0, tile] = lax.dot_general(
            hit_cols, weighted, (((1,), (1,)), ((), ())),
            precision=lax.Precision.HIGHEST, preferred_element_type=jnp.float32,
        )

    surface(1)

    lanes = lax.broadcasted_iota(jnp.int32, (cols, depth), 1)

    def advance(s, t, extra):
        now, new = fields[s][t], fields[s][t + 1]

        def one_row(at, tile, i):
            centre = now[at, tile_cols, :]
            total = 3.0 * stencil_weights[0] * centre
            for reach in range(1, 5):
                up = jnp.where(lanes >= reach, pltpu.roll(centre, reach, 1), 0.0)
                down = jnp.where(
                    lanes < depth - reach, pltpu.roll(centre, depth - reach, 1), 0.0)
                total = total + stencil_weights[reach] * (
                    (now[at + reach, tile_cols, :] + now[at - reach, tile_cols, :])
                    + (now[at, pl.ds(SIDE + reach, cols), :]
                       + now[at, pl.ds(SIDE - reach, cols), :])
                    + (up + down))
            shift = lax.rem(receiver_depth - (t * rows + i) + 2 * depth, depth)
            injected = jnp.where(
                lanes == receiver_depth, pltpu.roll(surf[s, tile], shift, 1), 0.0)
            before = older0[i] if t == 0 else fields[s][t - 1][at, tile_cols, :]
            new[at, tile_cols, :] = 2.0 * centre - before + vel2[at] * (total + injected)

        def some_rows(b, carry):
            begin = REACH - extra + b * 4
            tile = begin // rows
            for i in range(4):
                one_row(begin + i, tile, begin - tile * rows + i)
            return carry

        lax.fori_loop(0, (rows + 2 * extra) // 4, some_rows, 0)

    own_count = NLAG // shots
    first_lag = me_shot * own_count

    def correlate(t):
        last = t == steps

        def one_row(i, carry):
            sources = [src[s, t - 1, i] for s in range(shots)]
            for k in range(own_count):
                lag = lags[first_lag + k]
                at = REACH + i + lag
                total = sources[0] * fields[0][t][at, tile_cols, :]
                for s in range(1, shots):
                    total = total + sources[s] * fields[s][t][at, tile_cols, :]
                if t > 1:
                    total = out[k, i] + total
                if last:
                    total = total * jnp.abs(lag).astype(jnp.float32)
                out[k, i] = total
            return carry

        lax.fori_loop(0, rows, one_row, 0)

    await_recv(j_tile(0, 0))
    await_recv(z_near(0, 0))
    advance(0, 0, 0)
    start(z_near(0, 1))
    start(j_tile(0, 1))
    start(z_far(0, 1))
    to_shots(field_copy, 1)
    surface(0)
    surface(2)
    to_shots(surf_copy)
    mute(1)
    to_shots(src_copy, 1)
    await_recv(j_tile(0, 1))
    await_recv(z_near(0, 1))
    advance(0, 1, 0)
    start(z_near(0, 2))
    start(z_far(0, 2))
    to_shots(field_copy, 2)
    for t in range(2, steps):
        mute(t)
        to_shots(src_copy, t)

    for t in (1, 2):
        for s in range(1, shots):
            field_copy(shots - s, t).wait_recv()
            start(z_near(s, t))
            start(z_far(s, t))
    await_recv(z_far(0, 1))
    await_recv(z_near(0, 2))
    await_recv(z_far(0, 2))
    start(j_wide(0, 2))
    await_recv(z_vel())

    for t in range(2, steps):
        for s in range(shots):
            if t == 2 and s > 0:
                for early in (1, 2):
                    await_recv(z_near(s, early))
                    await_recv(z_far(s, early))
                start(j_wide(s, t))
                surf_copy(shots - s).wait_recv()
            await_recv(j_wide(s, t))
            if t > 2:
                await_recv(z_near(s, t))
            advance(s, t, EXTRA)
            start(z_near(s, t + 1))
            if t + 1 < steps:
                start(j_wide(s, t + 1))
        for s in range(1, shots):
            src_copy(shots - s, t - 2).wait_recv()
        correlate(t - 1)
    for t in (steps - 1, steps):
        for s in range(1, shots):
            src_copy(shots - s, t - 1).wait_recv()
        if t == steps:
            for s in range(shots):
                await_recv(z_near(s, t))
        correlate(t)

    for sends, _, copy in started:
        pl.when(sends)(copy.wait_send)
    for copy in shot_copies:
        copy.wait_send()


def on_device(
    sizes,
    vel2,
    adj_prev,
    adj_now,
    src_field,
    residual,
    rec_inline,
    rec_xline,
    src_inline,
    src_xline,
    lag_list,
):
    shots, _, _, rows, cols, depth, steps = sizes
    receivers = residual.shape[-1]
    anywhere = pl.BlockSpec(memory_space=pl.ANY)
    field = pltpu.VMEM((rows + 2 * REACH, cols + 2 * SIDE, depth), jnp.float32)
    dma = pltpu.SemaphoreType.DMA
    return pl.pallas_call(
        functools.partial(kernel, sizes),
        out_shape=jax.ShapeDtypeStruct((NLAG // shots, rows, cols, depth), jnp.float32),
        in_specs=[anywhere] * 10,
        out_specs=pl.BlockSpec(memory_space=pltpu.VMEM),
        scratch_shapes=[field] * (shots * (steps + 1)) + [
            pltpu.SMEM((NLAG,), jnp.int32),
            pltpu.SMEM((1,), jnp.int32),
            pltpu.SMEM((1,), jnp.int32),
            pltpu.VMEM((rows + 2 * REACH, cols, depth), jnp.float32),
            pltpu.VMEM((rows, cols, depth), jnp.float32),
            pltpu.VMEM((steps, receivers), jnp.float32),
            pltpu.VMEM((1, receivers), jnp.int32),
            pltpu.VMEM((1, receivers), jnp.int32),
            pltpu.VMEM((shots, steps, rows, cols, depth), jnp.float32),
            pltpu.VMEM((shots, 3, cols, steps * rows), jnp.float32),
            dma((10,)),
            dma((2,)), dma((2,)),
            dma((shots,)), dma((shots,)),
            dma((shots, 3)), dma((shots, 3)),
            dma((shots, steps)), dma((shots, steps)),
            dma((shots, steps + 1, 4)), dma((shots, steps + 1, 4)),
            dma((shots, steps + 1, 2)), dma((shots, steps + 1, 2)),
        ],
        compiler_params=pltpu.CompilerParams(
            collective_id=0, has_side_effects=True, vmem_limit_bytes=52 * 2**20),
        name="adjoint_window",
    )(lag_list, src_inline, src_xline, vel2, adj_prev, adj_now, residual, rec_inline, rec_xline,
      src_field)


def solution(mesh):
    in_specs = (
        P("inline", "xline", None),
        P(("group", "shot"), "inline", "xline", None),
        P(("group", "shot"), "inline", "xline", None),
        P(("group", "shot"), None, "inline", "xline", None),
        P(("group", "shot"), None, None),
        P(("group", "shot"), None),
        P(("group", "shot"), None),
        P(("group", "shot")),
        P(("group", "shot")),
        P(),
    )
    out_specs = P(("group", "shot"), "inline", "xline", None)

    def whole(vel2, adj_prev, adj_now, src_field, *rest):
        n_inline, n_xline = mesh.shape["inline"], mesh.shape["xline"]
        sizes = (mesh.shape["shot"], n_inline, n_xline, vel2.shape[0] // n_inline,
                 vel2.shape[1] // n_xline, vel2.shape[2], src_field.shape[1])
        return jax.shard_map(
            functools.partial(on_device, sizes), mesh=mesh, in_specs=in_specs,
            out_specs=out_specs, check_vma=False,
        )(vel2, adj_prev, adj_now, src_field, *rest)

    return whole
```

```python
import functools

import jax
import jax.numpy as jnp
from jax import lax
from jax.experimental import pallas as pl
from jax.experimental.pallas import tpu as pltpu
from jax.sharding import PartitionSpec as P

NLAG = 32
REACH = NLAG // 2
NEAR = 4
EXTRA = REACH - NEAR
SIDE = 8

stencil_weights = (-205.0 / 72.0, 8.0 / 5.0, -1.0 / 5.0, 8.0 / 315.0, -1.0 / 560.0)
mute_reach = 3
receiver_depth = 1
MESH = pl.DeviceIdType.MESH


def kernel(
    sizes,
    lags_in,
    src_at_inline_in,
    src_at_xline_in,
    vel2_in,
    adj_prev_in,
    adj_now_in,
    residual_in,
    rec_inline_in,
    rec_xline_in,
    src_field,
    out,
    *scratch,
):
    shots, n_inline, n_xline, rows, cols, depth, steps = sizes
    fields = [
        [scratch[s * (steps + 1) + t] for t in range(steps + 1)] for s in range(shots)
    ]
    (lags, src_at_inline, src_at_xline, vel2, older0, residual, rec_inline, rec_xline,
     src, surf, load_sem, vel_send, vel_recv, surf_send, surf_recv, now_send, now_recv,
     src_send, src_recv, z_send, z_recv, j_send, j_recv) = scratch[shots * (steps + 1):]
    me_shot = lax.axis_index("shot")
    me_in = lax.axis_index("inline")
    me_x = lax.axis_index("xline")
    has_low, has_high = me_in > 0, me_in < n_inline - 1
    has_left, has_right = me_x > 0, me_x < n_xline - 1
    tile_rows = pl.ds(REACH, rows)
    tile_cols = pl.ds(SIDE, cols)

    loads = [
        pltpu.make_async_copy(src_ref, dst_ref, load_sem.at[n])
        for n, (src_ref, dst_ref) in enumerate([
            (adj_now_in.at[0], fields[0][0].at[tile_rows, tile_cols, :]),
            (adj_prev_in.at[0], older0),
            (vel2_in, vel2.at[tile_rows]),
            (residual_in.at[0], residual),
            (rec_inline_in, rec_inline),
            (rec_xline_in, rec_xline),
            (src_field.at[0], src.at[0]),
            (lags_in, lags),
            (src_at_inline_in, src_at_inline),
            (src_at_xline_in, src_at_xline),
        ])
    ]
    for load in loads:
        load.start()

    def partner(d):
        return {"shot": lax.rem(me_shot + d, shots)}

    barrier = pltpu.get_barrier_semaphore()

    def greet(where):
        pl.semaphore_signal(barrier, inc=1, device_id=where, device_id_type=MESH)

    @pl.when(has_low)
    def _():
        greet({"inline": me_in - 1})

    @pl.when(has_high)
    def _():
        greet({"inline": me_in + 1})

    @pl.when(has_left)
    def _():
        greet({"xline": me_x - 1})

    @pl.when(has_right)
    def _():
        greet({"xline": me_x + 1})

    for d in range(1, shots):
        greet(partner(d))

    def z_copy(s, t, which, here, there, count, step_to):
        ref = fields[s][t]
        return pltpu.make_async_remote_copy(
            src_ref=ref.at[pl.ds(here, count), tile_cols, :],
            dst_ref=ref.at[pl.ds(there, count), tile_cols, :],
            send_sem=z_send.at[s, t, which],
            recv_sem=z_recv.at[s, t, which],
            device_id={"inline": me_in + step_to},
            device_id_type=MESH,
        )

    def z_rows(s, t, which, begin, end):
        return [
            (has_low, has_high,
             z_copy(s, t, which, REACH + begin, REACH + rows + begin, end - begin, -1)),
            (has_high, has_low,
             z_copy(s, t, which + 1, REACH + rows - end, REACH - end, end - begin, 1)),
        ]

    def z_near(s, t):
        if t >= 3:
            return z_rows(s, t, 0, EXTRA, REACH)
        return z_rows(s, t, 0, 0, NEAR)

    def z_far(s, t):
        return z_rows(s, t, 2, NEAR, REACH)

    def z_vel():
        def one(which, here, there, step_to):
            return pltpu.make_async_remote_copy(
                src_ref=vel2.at[pl.ds(here, EXTRA)], dst_ref=vel2.at[pl.ds(there, EXTRA)],
                send_sem=vel_send.at[which], recv_sem=vel_recv.at[which],
                device_id={"inline": me_in + step_to}, device_id_type=MESH)

        return [(has_low, has_high, one(0, REACH, REACH + rows, -1)),
                (has_high, has_low, one(1, REACH + rows - EXTRA, REACH - EXTRA, 1))]

    def j_copy(s, t, which, begin, count):
        ref = fields[s][t]
        some_rows = pl.ds(begin, count)
        left = pltpu.make_async_remote_copy(
            src_ref=ref.at[some_rows, pl.ds(SIDE, SIDE), :],
            dst_ref=ref.at[some_rows, pl.ds(SIDE + cols, SIDE), :],
            send_sem=j_send.at[s, t, which],
            recv_sem=j_recv.at[s, t, which],
            device_id={"xline": me_x - 1},
            device_id_type=MESH,
        )
        right = pltpu.make_async_remote_copy(
            src_ref=ref.at[some_rows, pl.ds(cols, SIDE), :],
            dst_ref=ref.at[some_rows, pl.ds(0, SIDE), :],
            send_sem=j_send.at[s, t, which + 1],
            recv_sem=j_recv.at[s, t, which + 1],
            device_id={"xline": me_x + 1},
            device_id_type=MESH,
        )
        return [(has_left, has_right, left), (has_right, has_left, right)]

    def j_tile(s, t):
        return j_copy(s, t, 0, REACH, rows)

    def j_inner(s, t):
        return j_copy(s, t, 0, REACH - EXTRA + NEAR, rows + 2 * (EXTRA - NEAR))

    def j_outer(s, t):
        return (j_copy(s, t, 2, REACH - EXTRA, NEAR)
                + j_copy(s, t, 4, REACH + rows + EXTRA - NEAR, NEAR))

    started = []

    def start(copies):
        for sends, _, copy in copies:
            pl.when(sends)(copy.start)
        started.extend(copies)

    def await_recv(copies):
        for _, receives, copy in copies:
            pl.when(receives)(copy.wait_recv)

    shot_copies = []

    def to_shot(d, src_ref, dst_ref, send_sem, recv_sem):
        return pltpu.make_async_remote_copy(
            src_ref=src_ref, dst_ref=dst_ref, send_sem=send_sem, recv_sem=recv_sem,
            device_id=partner(d), device_id_type=MESH,
        )

    def field_copy(d, t):
        return to_shot(
            d, fields[0][t].at[tile_rows, tile_cols, :],
            fields[shots - d][t].at[tile_rows, tile_cols, :],
            now_send.at[d, t], now_recv.at[shots - d, t])

    def surf_copy(d):
        return to_shot(d, surf.at[0], surf.at[shots - d], surf_send.at[d],
                       surf_recv.at[shots - d])

    def src_copy(d, t):
        return to_shot(d, src.at[0, t], src.at[shots - d, t], src_send.at[d, t],
                       src_recv.at[shots - d, t])

    def to_shots(copy_of, *what):
        for d in range(1, shots):
            copy = copy_of(d, *what)
            copy.start()
            shot_copies.append(copy)

    @pl.when(jnp.logical_not(has_low))
    def _():
        zero = jnp.zeros((REACH, cols, depth), jnp.float32)
        vel2[0:REACH] = zero
        fields[0][0][0:REACH, tile_cols, :] = zero
        for s in range(shots):
            for t in range(1, steps + 1):
                upto = REACH if t < 3 else REACH - EXTRA
                fields[s][t][0:upto, tile_cols, :] = zero[:upto]

    @pl.when(jnp.logical_not(has_high))
    def _():
        zero = jnp.zeros((REACH, cols, depth), jnp.float32)
        vel2[pl.ds(REACH + rows, REACH)] = zero
        fields[0][0][pl.ds(REACH + rows, REACH), tile_cols, :] = zero
        for s in range(shots):
            for t in range(1, steps + 1):
                upto = REACH if t < 3 else REACH - EXTRA
                fields[s][t][pl.ds(2 * REACH + rows - upto, upto), tile_cols, :] = zero[:upto]

    def zero_side(begin):
        zero = jnp.zeros((rows + 2 * EXTRA, SIDE, depth), jnp.float32)
        for s in range(shots):
            for t in range(steps):
                fields[s][t][pl.ds(REACH - EXTRA, rows + 2 * EXTRA), pl.ds(begin, SIDE), :] = zero

    @pl.when(jnp.logical_not(has_left))
    def _():
        zero_side(0)

    @pl.when(jnp.logical_not(has_right))
    def _():
        zero_side(SIDE + cols)

    pl.semaphore_wait(
        barrier,
        has_low.astype(jnp.int32) + has_high.astype(jnp.int32)
        + has_left.astype(jnp.int32) + has_right.astype(jnp.int32) + (shots - 1),
    )
    loads[0].wait()
    start(z_near(0, 0))
    start(j_tile(0, 0))

    for load in loads[6:]:
        load.wait()
    at_inline, at_xline = src_at_inline[0], src_at_xline[0]
    cell_cols = me_x * cols + lax.broadcasted_iota(jnp.int32, (cols, depth), 0)
    col_inside = (jnp.abs(cell_cols - at_xline) <= mute_reach).astype(jnp.float32)

    def mute(t):
        def mute_row(i, carry):
            hit = (jnp.abs(me_in * rows + i - at_inline) <= mute_reach).astype(jnp.float32)
            src[0, t, i] = src[0, t, i] * (1.0 - hit * col_inside)
            return carry

        lax.fori_loop(0, rows, mute_row, 0)

    mute(0)
    to_shots(src_copy, 0)
    for load in loads[1:6]:
        load.wait()

    col_ids = me_x * cols + lax.broadcasted_iota(jnp.int32, (cols, 1), 0)
    hit_cols = (rec_xline[...] == col_ids).astype(jnp.float32)

    def surface(tile):
        row_ids = (me_in + tile - 1) * rows + lax.broadcasted_iota(jnp.int32, (rows, 1), 0)
        hit_rows = (rec_inline[...] == row_ids).astype(jnp.float32)
        weighted = jnp.concatenate(
            [hit_rows * residual[t : t + 1, :] for t in range(steps)], axis=0
        )
        surf[0, tile] = lax.dot_general(
            hit_cols, weighted, (((1,), (1,)), ((), ())),
            precision=lax.Precision.HIGHEST, preferred_element_type=jnp.float32,
        )

    surface(1)

    lanes = lax.broadcasted_iota(jnp.int32, (cols, depth), 1)

    def advance(s, t, begin_row, end_row):
        now, new = fields[s][t], fields[s][t + 1]

        def one_row(at, tile, i):
            centre = now[at, tile_cols, :]
            total = 3.0 * stencil_weights[0] * centre
            for reach in range(1, 5):
                up = jnp.where(lanes >= reach, pltpu.roll(centre, reach, 1), 0.0)
                down = jnp.where(
                    lanes < depth - reach, pltpu.roll(centre, depth - reach, 1), 0.0)
                total = total + stencil_weights[reach] * (
                    (now[at + reach, tile_cols, :] + now[at - reach, tile_cols, :])
                    + (now[at, pl.ds(SIDE + reach, cols), :]
                       + now[at, pl.ds(SIDE - reach, cols), :])
                    + (up + down))
            shift = lax.rem(receiver_depth - (t * rows + i) + 2 * depth, depth)
            injected = jnp.where(
                lanes == receiver_depth, pltpu.roll(surf[s, tile], shift, 1), 0.0)
            before = older0[i] if t == 0 else fields[s][t - 1][at, tile_cols, :]
            new[at, tile_cols, :] = 2.0 * centre - before + vel2[at] * (total + injected)

        def some_rows(b, carry):
            begin = b * 4
            tile = begin // rows
            for i in range(4):
                one_row(begin + i, tile, begin - tile * rows + i)
            return carry

        lax.fori_loop(begin_row // 4, end_row // 4, some_rows, 0)

    own_count = NLAG // shots
    first_lag = me_shot * own_count

    def correlate(t):
        last = t == steps

        def one_row(i, carry):
            sources = [src[s, t - 1, i] for s in range(shots)]
            for k in range(own_count):
                lag = lags[first_lag + k]
                at = REACH + i + lag
                total = sources[0] * fields[0][t][at, tile_cols, :]
                for s in range(1, shots):
                    total = total + sources[s] * fields[s][t][at, tile_cols, :]
                if t > 1:
                    total = out[k, i] + total
                if last:
                    total = total * jnp.abs(lag).astype(jnp.float32)
                out[k, i] = total
            return carry

        lax.fori_loop(0, rows, one_row, 0)

    await_recv(j_tile(0, 0))
    await_recv(z_near(0, 0))
    advance(0, 0, REACH, REACH + rows)
    start(z_near(0, 1))
    start(j_tile(0, 1))
    start(z_far(0, 1))
    to_shots(field_copy, 1)
    surface(0)
    surface(2)
    to_shots(surf_copy)
    await_recv(j_tile(0, 1))
    await_recv(z_near(0, 1))
    advance(0, 1, REACH, REACH + rows)
    start(z_near(0, 2))
    start(z_far(0, 2))
    to_shots(field_copy, 2)
    start(z_vel())
    for t in range(1, steps):
        mute(t)

    for t in (1, 2):
        for s in range(1, shots):
            field_copy(shots - s, t).wait_recv()
            start(z_near(s, t))
            start(z_far(s, t))
    for t in range(1, steps):
        to_shots(src_copy, t)
    await_recv(z_far(0, 1))
    await_recv(z_near(0, 2))
    await_recv(z_far(0, 2))
    start(j_inner(0, 2))
    start(j_outer(0, 2))
    await_recv(z_vel())

    for t in range(2, steps):
        for s in range(shots):
            if t == 2 and s > 0:
                for early in (1, 2):
                    await_recv(z_near(s, early))
                    await_recv(z_far(s, early))
                start(j_inner(s, t))
                start(j_outer(s, t))
                surf_copy(shots - s).wait_recv()
            await_recv(j_inner(s, t))
            low, high = REACH - EXTRA, REACH + rows + EXTRA
            advance(s, t, REACH, REACH + NEAR)
            advance(s, t, REACH + rows - NEAR, REACH + rows)
            start(z_near(s, t + 1))
            advance(s, t, low + NEAR, REACH)
            advance(s, t, REACH + NEAR, REACH + rows - NEAR)
            advance(s, t, REACH + rows, high - NEAR)
            if t + 1 < steps:
                start(j_inner(s, t + 1))
            await_recv(j_outer(s, t))
            if t > 2:
                await_recv(z_near(s, t))
            advance(s, t, low, low + NEAR)
            advance(s, t, high - NEAR, high)
            if t + 1 < steps:
                start(j_outer(s, t + 1))
        for s in range(1, shots):
            src_copy(shots - s, t - 2).wait_recv()
        correlate(t - 1)
    for t in (steps - 1, steps):
        for s in range(1, shots):
            src_copy(shots - s, t - 1).wait_recv()
        if t == steps:
            for s in range(shots):
                await_recv(z_near(s, t))
        correlate(t)

    for sends, _, copy in started:
        pl.when(sends)(copy.wait_send)
    for copy in shot_copies:
        copy.wait_send()


def on_device(
    sizes,
    vel2,
    adj_prev,
    adj_now,
    src_field,
    residual,
    rec_inline,
    rec_xline,
    src_inline,
    src_xline,
    lag_list,
):
    shots, _, _, rows, cols, depth, steps = sizes
    receivers = residual.shape[-1]
    anywhere = pl.BlockSpec(memory_space=pl.ANY)
    field = pltpu.VMEM((rows + 2 * REACH, cols + 2 * SIDE, depth), jnp.float32)
    dma = pltpu.SemaphoreType.DMA
    return pl.pallas_call(
        functools.partial(kernel, sizes),
        out_shape=jax.ShapeDtypeStruct((NLAG // shots, rows, cols, depth), jnp.float32),
        in_specs=[anywhere] * 10,
        out_specs=pl.BlockSpec(memory_space=pltpu.VMEM),
        scratch_shapes=[field] * (shots * (steps + 1)) + [
            pltpu.SMEM((NLAG,), jnp.int32),
            pltpu.SMEM((1,), jnp.int32),
            pltpu.SMEM((1,), jnp.int32),
            pltpu.VMEM((rows + 2 * REACH, cols, depth), jnp.float32),
            pltpu.VMEM((rows, cols, depth), jnp.float32),
            pltpu.VMEM((steps, receivers), jnp.float32),
            pltpu.VMEM((1, receivers), jnp.int32),
            pltpu.VMEM((1, receivers), jnp.int32),
            pltpu.VMEM((shots, steps, rows, cols, depth), jnp.float32),
            pltpu.VMEM((shots, 3, cols, steps * rows), jnp.float32),
            dma((10,)),
            dma((2,)), dma((2,)),
            dma((shots,)), dma((shots,)),
            dma((shots, 3)), dma((shots, 3)),
            dma((shots, steps)), dma((shots, steps)),
            dma((shots, steps + 1, 4)), dma((shots, steps + 1, 4)),
            dma((shots, steps + 1, 6)), dma((shots, steps + 1, 6)),
        ],
        compiler_params=pltpu.CompilerParams(
            collective_id=0, has_side_effects=True, vmem_limit_bytes=63 * 2**20),
        name="adjoint_window",
    )(lag_list, src_inline, src_xline, vel2, adj_prev, adj_now, residual, rec_inline, rec_xline,
      src_field)


def solution(mesh):
    in_specs = (
        P("inline", "xline", None),
        P(("group", "shot"), "inline", "xline", None),
        P(("group", "shot"), "inline", "xline", None),
        P(("group", "shot"), None, "inline", "xline", None),
        P(("group", "shot"), None, None),
        P(("group", "shot"), None),
        P(("group", "shot"), None),
        P(("group", "shot")),
        P(("group", "shot")),
        P(),
    )
    out_specs = P(("group", "shot"), "inline", "xline", None)

    def whole(vel2, adj_prev, adj_now, src_field, *rest):
        n_inline, n_xline = mesh.shape["inline"], mesh.shape["xline"]
        sizes = (mesh.shape["shot"], n_inline, n_xline, vel2.shape[0] // n_inline,
                 vel2.shape[1] // n_xline, vel2.shape[2], src_field.shape[1])
        return jax.shard_map(
            functools.partial(on_device, sizes), mesh=mesh, in_specs=in_specs,
            out_specs=out_specs, check_vma=False,
        )(vel2, adj_prev, adj_now, src_field, *rest)

    return whole
```

```python
import functools

import jax
import jax.numpy as jnp
from jax import lax
from jax.experimental import pallas as pl
from jax.experimental.pallas import tpu as pltpu
from jax.sharding import PartitionSpec as P

NLAG = 32
REACH = NLAG // 2
NEAR = 4
EXTRA = REACH - NEAR
SIDE = 8

stencil_weights = (-205.0 / 72.0, 8.0 / 5.0, -1.0 / 5.0, 8.0 / 315.0, -1.0 / 560.0)
mute_reach = 3
receiver_depth = 1
MESH = pl.DeviceIdType.MESH


def kernel(
    sizes,
    lags_in,
    src_at_inline_in,
    src_at_xline_in,
    vel2_in,
    adj_prev_in,
    adj_now_in,
    residual_in,
    rec_inline_in,
    rec_xline_in,
    src_field,
    out,
    *scratch,
):
    shots, n_inline, n_xline, rows, cols, depth, steps = sizes
    fields = [
        [scratch[s * (steps + 1) + t] for t in range(steps + 1)] for s in range(shots)
    ]
    (lags, src_at_inline, src_at_xline, vel2, older0, residual, rec_inline, rec_xline,
     src, surf, load_sem, vel_send, vel_recv, surf_send, surf_recv, now_send, now_recv,
     src_send, src_recv, z_send, z_recv, j_send, j_recv) = scratch[shots * (steps + 1):]
    me_shot = lax.axis_index("shot")
    me_in = lax.axis_index("inline")
    me_x = lax.axis_index("xline")
    has_low, has_high = me_in > 0, me_in < n_inline - 1
    has_left, has_right = me_x > 0, me_x < n_xline - 1
    tile_rows = pl.ds(REACH, rows)
    tile_cols = pl.ds(SIDE, cols)

    loads = [
        pltpu.make_async_copy(src_ref, dst_ref, load_sem.at[n])
        for n, (src_ref, dst_ref) in enumerate([
            (adj_now_in.at[0], fields[0][0].at[tile_rows, tile_cols, :]),
            (adj_prev_in.at[0], older0),
            (vel2_in, vel2.at[tile_rows]),
            (residual_in.at[0], residual),
            (rec_inline_in, rec_inline),
            (rec_xline_in, rec_xline),
            (src_field.at[0], src.at[0]),
            (lags_in, lags),
            (src_at_inline_in, src_at_inline),
            (src_at_xline_in, src_at_xline),
        ])
    ]
    for load in loads:
        load.start()

    def partner(d):
        return {"shot": lax.rem(me_shot + d, shots)}

    barrier = pltpu.get_barrier_semaphore()

    def greet(where):
        pl.semaphore_signal(barrier, inc=1, device_id=where, device_id_type=MESH)

    @pl.when(has_low)
    def _():
        greet({"inline": me_in - 1})

    @pl.when(has_high)
    def _():
        greet({"inline": me_in + 1})

    @pl.when(has_left)
    def _():
        greet({"xline": me_x - 1})

    @pl.when(has_right)
    def _():
        greet({"xline": me_x + 1})

    for d in range(1, shots):
        greet(partner(d))

    def z_copy(s, t, which, here, there, count, step_to):
        ref = fields[s][t]
        return pltpu.make_async_remote_copy(
            src_ref=ref.at[pl.ds(here, count), tile_cols, :],
            dst_ref=ref.at[pl.ds(there, count), tile_cols, :],
            send_sem=z_send.at[s, t, which],
            recv_sem=z_recv.at[s, t, which],
            device_id={"inline": me_in + step_to},
            device_id_type=MESH,
        )

    def z_rows(s, t, which, begin, end):
        return [
            (has_low, has_high,
             z_copy(s, t, which, REACH + begin, REACH + rows + begin, end - begin, -1)),
            (has_high, has_low,
             z_copy(s, t, which + 1, REACH + rows - end, REACH - end, end - begin, 1)),
        ]

    def z_near(s, t):
        if t >= 3:
            return z_rows(s, t, 0, EXTRA, REACH)
        return z_rows(s, t, 0, 0, NEAR)

    def z_far(s, t):
        return z_rows(s, t, 2, NEAR, REACH)

    def z_vel():
        def one(which, here, there, step_to):
            return pltpu.make_async_remote_copy(
                src_ref=vel2.at[pl.ds(here, EXTRA)], dst_ref=vel2.at[pl.ds(there, EXTRA)],
                send_sem=vel_send.at[which], recv_sem=vel_recv.at[which],
                device_id={"inline": me_in + step_to}, device_id_type=MESH)

        return [(has_low, has_high, one(0, REACH, REACH + rows, -1)),
                (has_high, has_low, one(1, REACH + rows - EXTRA, REACH - EXTRA, 1))]

    def j_copy(s, t, which, begin, count):
        ref = fields[s][t]
        some_rows = pl.ds(begin, count)
        left = pltpu.make_async_remote_copy(
            src_ref=ref.at[some_rows, pl.ds(SIDE, SIDE), :],
            dst_ref=ref.at[some_rows, pl.ds(SIDE + cols, SIDE), :],
            send_sem=j_send.at[s, t, which],
            recv_sem=j_recv.at[s, t, which],
            device_id={"xline": me_x - 1},
            device_id_type=MESH,
        )
        right = pltpu.make_async_remote_copy(
            src_ref=ref.at[some_rows, pl.ds(cols, SIDE), :],
            dst_ref=ref.at[some_rows, pl.ds(0, SIDE), :],
            send_sem=j_send.at[s, t, which + 1],
            recv_sem=j_recv.at[s, t, which + 1],
            device_id={"xline": me_x + 1},
            device_id_type=MESH,
        )
        return [(has_left, has_right, left), (has_right, has_left, right)]

    def j_tile(s, t):
        return j_copy(s, t, 0, REACH, rows)

    def j_inner(s, t):
        return j_copy(s, t, 0, REACH - EXTRA + NEAR, rows + 2 * (EXTRA - NEAR))

    def j_outer(s, t):
        return (j_copy(s, t, 2, REACH - EXTRA, NEAR)
                + j_copy(s, t, 4, REACH + rows + EXTRA - NEAR, NEAR))

    started = []

    def start(copies):
        for sends, _, copy in copies:
            pl.when(sends)(copy.start)
        started.extend(copies)

    def await_recv(copies):
        for _, receives, copy in copies:
            pl.when(receives)(copy.wait_recv)

    shot_copies = []

    def to_shot(d, src_ref, dst_ref, send_sem, recv_sem):
        return pltpu.make_async_remote_copy(
            src_ref=src_ref, dst_ref=dst_ref, send_sem=send_sem, recv_sem=recv_sem,
            device_id=partner(d), device_id_type=MESH,
        )

    def field_copy(d, t):
        return to_shot(
            d, fields[0][t].at[tile_rows, tile_cols, :],
            fields[shots - d][t].at[tile_rows, tile_cols, :],
            now_send.at[d, t], now_recv.at[shots - d, t])

    def surf_copy(d):
        return to_shot(d, surf.at[0], surf.at[shots - d], surf_send.at[d],
                       surf_recv.at[shots - d])

    def src_copy(d, t):
        return to_shot(d, src.at[0, t], src.at[shots - d, t], src_send.at[d, t],
                       src_recv.at[shots - d, t])

    def to_shots(copy_of, *what):
        for d in range(1, shots):
            copy = copy_of(d, *what)
            copy.start()
            shot_copies.append(copy)

    @pl.when(jnp.logical_not(has_low))
    def _():
        zero = jnp.zeros((REACH, cols, depth), jnp.float32)
        vel2[0:REACH] = zero
        fields[0][0][0:REACH, tile_cols, :] = zero
        for s in range(shots):
            for t in range(1, steps + 1):
                upto = REACH if t < 3 else REACH - EXTRA
                fields[s][t][0:upto, tile_cols, :] = zero[:upto]

    @pl.when(jnp.logical_not(has_high))
    def _():
        zero = jnp.zeros((REACH, cols, depth), jnp.float32)
        vel2[pl.ds(REACH + rows, REACH)] = zero
        fields[0][0][pl.ds(REACH + rows, REACH), tile_cols, :] = zero
        for s in range(shots):
            for t in range(1, steps + 1):
                upto = REACH if t < 3 else REACH - EXTRA
                fields[s][t][pl.ds(2 * REACH + rows - upto, upto), tile_cols, :] = zero[:upto]

    def zero_side(begin):
        zero = jnp.zeros((rows + 2 * EXTRA, SIDE, depth), jnp.float32)
        for s in range(shots):
            for t in range(steps):
                fields[s][t][pl.ds(REACH - EXTRA, rows + 2 * EXTRA), pl.ds(begin, SIDE), :] = zero

    @pl.when(jnp.logical_not(has_left))
    def _():
        zero_side(0)

    @pl.when(jnp.logical_not(has_right))
    def _():
        zero_side(SIDE + cols)

    pl.semaphore_wait(
        barrier,
        has_low.astype(jnp.int32) + has_high.astype(jnp.int32)
        + has_left.astype(jnp.int32) + has_right.astype(jnp.int32) + (shots - 1),
    )
    loads[0].wait()
    start(z_near(0, 0))
    start(j_tile(0, 0))

    for load in loads[6:]:
        load.wait()
    at_inline, at_xline = src_at_inline[0], src_at_xline[0]
    cell_cols = me_x * cols + lax.broadcasted_iota(jnp.int32, (cols, depth), 0)
    col_inside = (jnp.abs(cell_cols - at_xline) <= mute_reach).astype(jnp.float32)

    def mute(t):
        def mute_row(i, carry):
            hit = (jnp.abs(me_in * rows + i - at_inline) <= mute_reach).astype(jnp.float32)
            src[0, t, i] = src[0, t, i] * (1.0 - hit * col_inside)
            return carry

        lax.fori_loop(0, rows, mute_row, 0)

    mute(0)
    to_shots(src_copy, 0)
    for load in loads[1:6]:
        load.wait()

    col_ids = me_x * cols + lax.broadcasted_iota(jnp.int32, (cols, 1), 0)
    hit_cols = (rec_xline[...] == col_ids).astype(jnp.float32)

    def surface(tile):
        row_ids = (me_in + tile - 1) * rows + lax.broadcasted_iota(jnp.int32, (rows, 1), 0)
        hit_rows = (rec_inline[...] == row_ids).astype(jnp.float32)
        weighted = jnp.concatenate(
            [hit_rows * residual[t : t + 1, :] for t in range(steps)], axis=0
        )
        surf[0, tile] = lax.dot_general(
            hit_cols, weighted, (((1,), (1,)), ((), ())),
            precision=lax.Precision.HIGHEST, preferred_element_type=jnp.float32,
        )

    surface(1)

    lanes = lax.broadcasted_iota(jnp.int32, (cols, depth), 1)

    def advance(s, t, blocks, begin_of):
        now, new = fields[s][t], fields[s][t + 1]

        def one_row(at, tile, i):
            centre = now[at, tile_cols, :]
            total = 3.0 * stencil_weights[0] * centre
            for reach in range(1, 5):
                up = jnp.where(lanes >= reach, pltpu.roll(centre, reach, 1), 0.0)
                down = jnp.where(
                    lanes < depth - reach, pltpu.roll(centre, depth - reach, 1), 0.0)
                total = total + stencil_weights[reach] * (
                    (now[at + reach, tile_cols, :] + now[at - reach, tile_cols, :])
                    + (now[at, pl.ds(SIDE + reach, cols), :]
                       + now[at, pl.ds(SIDE - reach, cols), :])
                    + (up + down))
            shift = lax.rem(receiver_depth - (t * rows + i) + 2 * depth, depth)
            injected = jnp.where(
                lanes == receiver_depth, pltpu.roll(surf[s, tile], shift, 1), 0.0)
            before = older0[i] if t == 0 else fields[s][t - 1][at, tile_cols, :]
            new[at, tile_cols, :] = 2.0 * centre - before + vel2[at] * (total + injected)

        def some_rows(b, carry):
            begin = begin_of(b)
            tile = begin // rows
            for i in range(4):
                one_row(begin + i, tile, begin - tile * rows + i)
            return carry

        lax.fori_loop(0, blocks, some_rows, 0)

    own_count = NLAG // shots
    first_lag = me_shot * own_count

    def correlate(t):
        last = t == steps

        def one_row(i, carry):
            sources = [src[s, t - 1, i] for s in range(shots)]
            for k in range(own_count):
                lag = lags[first_lag + k]
                at = REACH + i + lag
                total = sources[0] * fields[0][t][at, tile_cols, :]
                for s in range(1, shots):
                    total = total + sources[s] * fields[s][t][at, tile_cols, :]
                if t > 1:
                    total = out[k, i] + total
                if last:
                    total = total * jnp.abs(lag).astype(jnp.float32)
                out[k, i] = total
            return carry

        lax.fori_loop(0, rows, one_row, 0)

    await_recv(j_tile(0, 0))
    await_recv(z_near(0, 0))
    advance(0, 0, rows // 4, lambda b: REACH + 4 * b)
    start(z_near(0, 1))
    start(j_tile(0, 1))
    start(z_far(0, 1))
    to_shots(field_copy, 1)
    surface(0)
    surface(2)
    to_shots(surf_copy)
    await_recv(j_tile(0, 1))
    await_recv(z_near(0, 1))
    advance(0, 1, rows // 4, lambda b: REACH + 4 * b)
    start(z_near(0, 2))
    start(z_far(0, 2))
    to_shots(field_copy, 2)
    start(z_vel())
    for t in range(1, steps):
        mute(t)

    for t in (1, 2):
        for s in range(1, shots):
            field_copy(shots - s, t).wait_recv()
            start(z_near(s, t))
            start(z_far(s, t))
    for t in range(1, steps):
        to_shots(src_copy, t)
    await_recv(z_far(0, 1))
    await_recv(z_near(0, 2))
    await_recv(z_far(0, 2))
    start(j_inner(0, 2))
    start(j_outer(0, 2))
    await_recv(z_vel())

    for t in range(2, steps):
        for s in range(shots):
            if t == 2 and s > 0:
                for early in (1, 2):
                    await_recv(z_near(s, early))
                    await_recv(z_far(s, early))
                start(j_inner(s, t))
                start(j_outer(s, t))
                surf_copy(shots - s).wait_recv()
            await_recv(j_inner(s, t))
            low, high = REACH - EXTRA, REACH + rows + EXTRA
            advance(s, t, 2, lambda b: REACH + b * (rows - NEAR))
            start(z_near(s, t + 1))
            advance(s, t, 6, lambda b: low + NEAR + 4 * b + 4 * (b // 2))
            if t + 1 < steps:
                start(j_inner(s, t + 1))
            await_recv(j_outer(s, t))
            if t > 2:
                await_recv(z_near(s, t))
            advance(s, t, 2, lambda b: low + b * (high - NEAR - low))
            if t + 1 < steps:
                start(j_outer(s, t + 1))
        for s in range(1, shots):
            src_copy(shots - s, t - 2).wait_recv()
        correlate(t - 1)
    for t in (steps - 1, steps):
        for s in range(1, shots):
            src_copy(shots - s, t - 1).wait_recv()
        if t == steps:
            for s in range(shots):
                await_recv(z_near(s, t))
        correlate(t)

    for sends, _, copy in started:
        pl.when(sends)(copy.wait_send)
    for copy in shot_copies:
        copy.wait_send()


def on_device(
    sizes,
    vel2,
    adj_prev,
    adj_now,
    src_field,
    residual,
    rec_inline,
    rec_xline,
    src_inline,
    src_xline,
    lag_list,
):
    shots, _, _, rows, cols, depth, steps = sizes
    receivers = residual.shape[-1]
    anywhere = pl.BlockSpec(memory_space=pl.ANY)
    field = pltpu.VMEM((rows + 2 * REACH, cols + 2 * SIDE, depth), jnp.float32)
    dma = pltpu.SemaphoreType.DMA
    return pl.pallas_call(
        functools.partial(kernel, sizes),
        out_shape=jax.ShapeDtypeStruct((NLAG // shots, rows, cols, depth), jnp.float32),
        in_specs=[anywhere] * 10,
        out_specs=pl.BlockSpec(memory_space=pltpu.VMEM),
        scratch_shapes=[field] * (shots * (steps + 1)) + [
            pltpu.SMEM((NLAG,), jnp.int32),
            pltpu.SMEM((1,), jnp.int32),
            pltpu.SMEM((1,), jnp.int32),
            pltpu.VMEM((rows + 2 * REACH, cols, depth), jnp.float32),
            pltpu.VMEM((rows, cols, depth), jnp.float32),
            pltpu.VMEM((steps, receivers), jnp.float32),
            pltpu.VMEM((1, receivers), jnp.int32),
            pltpu.VMEM((1, receivers), jnp.int32),
            pltpu.VMEM((shots, steps, rows, cols, depth), jnp.float32),
            pltpu.VMEM((shots, 3, cols, steps * rows), jnp.float32),
            dma((10,)),
            dma((2,)), dma((2,)),
            dma((shots,)), dma((shots,)),
            dma((shots, 3)), dma((shots, 3)),
            dma((shots, steps)), dma((shots, steps)),
            dma((shots, steps + 1, 4)), dma((shots, steps + 1, 4)),
            dma((shots, steps + 1, 6)), dma((shots, steps + 1, 6)),
        ],
        compiler_params=pltpu.CompilerParams(
            collective_id=0, has_side_effects=True, vmem_limit_bytes=63 * 2**20),
        name="adjoint_window",
    )(lag_list, src_inline, src_xline, vel2, adj_prev, adj_now, residual, rec_inline, rec_xline,
      src_field)


def solution(mesh):
    in_specs = (
        P("inline", "xline", None),
        P(("group", "shot"), "inline", "xline", None),
        P(("group", "shot"), "inline", "xline", None),
        P(("group", "shot"), None, "inline", "xline", None),
        P(("group", "shot"), None, None),
        P(("group", "shot"), None),
        P(("group", "shot"), None),
        P(("group", "shot")),
        P(("group", "shot")),
        P(),
    )
    out_specs = P(("group", "shot"), "inline", "xline", None)

    def whole(vel2, adj_prev, adj_now, src_field, *rest):
        n_inline, n_xline = mesh.shape["inline"], mesh.shape["xline"]
        sizes = (mesh.shape["shot"], n_inline, n_xline, vel2.shape[0] // n_inline,
                 vel2.shape[1] // n_xline, vel2.shape[2], src_field.shape[1])
        return jax.shard_map(
            functools.partial(on_device, sizes), mesh=mesh, in_specs=in_specs,
            out_specs=out_specs, check_vma=False,
        )(vel2, adj_prev, adj_now, src_field, *rest)

    return whole
```
